32 devices in a mesh: dp: 8 (over y, x, core), group: 4 (over z).
Axes of the slice: x: 2, y: 2, z: 4, core: 2. Of those that a mesh axis runs over, the one named last changes fastest.
Arguments:
- tokens: bfloat16 [32768, 768], P(('dp', 'group')), may hold values from -6 to 6
- cotangent: bfloat16 [32768, 768], P(('dp', 'group')), may hold values from -6 to 6
- seq_lens: int32 [32, 4], P(('dp', 'group')), may hold values from 0 to 1024, as said below
- w_qkv: float32 [1769472], P(('dp', 'group')), may hold values from -0.21875 to 0.21875
- w_out: float32 [589824], P(('dp', 'group')), may hold values from -1.75 to 1.75
- w_up: float32 [2359296], P(('dp', 'group')), may hold values from -0.21875 to 0.21875
- w_down: float32 [2359296], P(('dp', 'group')), may hold values from -0.109375 to 0.109375
- vectors: float32 [9984], P(('dp', 'group')), may hold values from -0.4 to 1.3, as said below
- first_qkv: float32 [1769472], P(('dp', 'group')), may hold values from -128 to 128
- first_out: float32 [589824], P(('dp', 'group')), may hold values from -12 to 12
- first_up: float32 [2359296], P(('dp', 'group')), may hold values from -32 to 32
- first_down: float32 [2359296], P(('dp', 'group')), may hold values from -64 to 64
- first_vec: float32 [9984], P(('dp', 'group')), may hold values from -256 to 256
- second_qkv: float32 [1769472], P(('dp', 'group')), may hold values from 16.384 to 262.144
- second_out: float32 [589824], P(('dp', 'group')), may hold values from 0.16384 to 2.62144
- second_up: float32 [2359296], P(('dp', 'group')), may hold values from 0.98304 to 16.384
- second_down: float32 [2359296], P(('dp', 'group')), may hold values from 4.096 to 65.536
- second_vec: float32 [9984], P(('dp', 'group')), may hold values from 65.536 to 1048.576
Outputs:
- block_out: bfloat16 [32768, 768], P(('dp', 'group'))
- input_grad: float32 [32768, 768], P(('dp', 'group'))
- new_w_qkv: float32 [1769472], P(('dp', 'group'))
- new_w_out: float32 [589824], P(('dp', 'group'))
- new_w_up: float32 [2359296], P(('dp', 'group'))
- new_w_down: float32 [2359296], P(('dp', 'group'))
- new_vectors: float32 [9984], P(('dp', 'group'))
- new_first_qkv: float32 [1769472], P(('dp', 'group'))
- new_first_out: float32 [589824], P(('dp', 'group'))
- new_first_up: float32 [2359296], P(('dp', 'group'))
- new_first_down: float32 [2359296], P(('dp', 'group'))
- new_first_vec: float32 [9984], P(('dp', 'group'))
- new_second_qkv: float32 [1769472], P(('dp', 'group'))
- new_second_out: float32 [589824], P(('dp', 'group'))
- new_second_up: float32 [2359296], P(('dp', 'group'))
- new_second_down: float32 [2359296], P(('dp', 'group'))
- new_second_vec: float32 [9984], P(('dp', 'group'))
The draws below stay inside these ranges and needn't reach their ends.
Inputs may be any that keep to these rules, and one draw needn't show every extreme that they name: `seq_lens`: row r lists, in order, the lengths of the sequences packed into the rows of device r of dp+group (dp slowest); its nonzero entries come first and sum to at most 1024; some row begins with a sequence of 1024 tokens and sums to exactly 1024. `vectors`: entries 0 to 2 * 768 - 1 (the gains) lie between 0.7 and 1.3; the others between -0.4 and 0.4.
All inputs are finite; a program needn't handle non-finite values.
Results may differ from the reference program's by a relative error of at most 0.012.
Values may be sent and summed in bfloat16 or wider, within the bound.
A program may use at most 192 MiB of HBM per device.

```python
import math
import jax
import jax.numpy as jnp
from jax import lax

D = 768
HEADS = 12
HEAD = 64
ROT = 16
FF = 3072
TOK_DEV = 1024
SEQ_MAX = 1024
STEP = 10
SLOTS = 4
SHARDS = 32
TOKENS = 32768


def draw_seq_lens(key, part):
    key = jax.random.fold_in(key, 7)
    key_pieces, key_counts, key_pick = jax.random.split(key, 3)
    pieces = jax.random.randint(key_pieces, (SHARDS, SLOTS), 1, SEQ_MAX + 1)
    counts = jax.random.randint(key_counts, (SHARDS,), TOK_DEV // 2, TOK_DEV + 1)
    chosen = jax.random.randint(key_pick, (), 0, SHARDS)
    picked = jnp.arange(SHARDS) == chosen
    pieces = jnp.where(picked[:, None], SEQ_MAX, pieces)
    counts = jnp.where(picked, TOK_DEV, counts)
    bounds = jnp.minimum(jnp.cumsum(pieces, axis=1), counts[:, None])
    starts = jnp.concatenate([jnp.zeros((SHARDS, 1), bounds.dtype), bounds[:, :-1]], axis=1)
    return (bounds - starts).astype(jnp.int32)


def draw_vectors(key, part):
    key = jax.random.fold_in(key, 5)
    key_gain, key_bias = jax.random.split(key)
    gains = jax.random.uniform(key_gain, (2 * D,), jnp.float32, 0.7, 1.3)
    biases = jax.random.uniform(key_bias, (7 * D + FF,), jnp.float32, -0.4, 0.4)
    return jnp.concatenate([gains, biases])


def block_levels(stream_key, extent, cuts, least, high):
    level, own = 1.0, jax.random.fold_in(stream_key, 6)
    for dim, shards_of in cuts:
        draws = jnp.exp(jax.random.uniform(jax.random.fold_in(own, dim), (shards_of,), jnp.float32, least / len(cuts), high / len(cuts)))
        level = level * jnp.repeat(draws, extent[dim] // shards_of).reshape([-1 if axis == dim else 1 for axis in range(len(extent))])
    return level


def gaussian(own_key, shape, width, bound, shards=(), held_as=jnp.bfloat16):
    values = jax.random.normal(own_key, shape, jnp.float32) * width
    if len(shards) > 0:
        values = block_levels(own_key, shape, shards, -0.22, 0.18) * values
    return jnp.clip(values, min=-bound, max=bound).astype(held_as)


def setup_inputs(seed: int = 0) -> dict:
    splits = jax.random.split(jax.random.key(seed), 19)
    return {
        "tokens": gaussian(splits[0], (TOKENS, D), 1.0, 6.0, ((0, 32),)),
        "cotangent": gaussian(splits[1], (TOKENS, D), 1.0, 6.0, ((0, 32),)),
        "seq_lens": draw_seq_lens(jax.random.fold_in(splits[18], 71), 0),
        "w_qkv": gaussian(splits[3], (3 * D * D,), D ** -0.5, 0.21875, ((0, 32),), jnp.float32),
        "w_out": gaussian(splits[4], (D * D,), (D * 16 // SEQ_MAX) ** -0.5, 1.75, ((0, 32),), jnp.float32),
        "w_up": gaussian(splits[5], (D * FF,), D ** -0.5, 0.21875, ((0, 32),), jnp.float32),
        "w_down": gaussian(splits[6], (FF * D,), FF ** -0.5, 0.109375, ((0, 32),), jnp.float32),
        "vectors": draw_vectors(jax.random.fold_in(splits[18], 71), 0),
        "first_qkv": gaussian(splits[8], (3 * D * D,), (0.11 * TOKENS ** 0.5), 128.0, ((0, 32),), jnp.float32),
        "first_out": gaussian(splits[9], (D * D,), (0.011 * TOKENS ** 0.5), 12.0, ((0, 32),), jnp.float32),
        "first_up": gaussian(splits[10], (D * FF,), (0.0275 * TOKENS ** 0.5), 32.0, ((0, 32),), jnp.float32),
        "first_down": gaussian(splits[11], (FF * D,), (0.055 * TOKENS ** 0.5), 64.0, ((0, 32),), jnp.float32),
        "first_vec": gaussian(splits[12], (9 * D + FF,), (0.22 * TOKENS ** 0.5), 256.0, ((0, 32),), jnp.float32),
        "second_qkv": jnp.clip(jnp.exp(math.log(262.144) - 2.7725887 * jax.random.uniform(splits[13], (3 * D * D,), jnp.float32) ** block_levels(splits[13], (3 * D * D,), ((0, 32),), -0.2, 0.2)), 16.384, 262.144),
        "second_out": jnp.clip(jnp.exp(math.log(2.62144) - 2.7725887 * jax.random.uniform(splits[14], (D * D,), jnp.float32) ** block_levels(splits[14], (D * D,), ((0, 32),), -0.2, 0.2)), 0.16384, 2.62144),
        "second_up": jnp.clip(jnp.exp(math.log(16.384) - 2.8134108 * jax.random.uniform(splits[15], (D * FF,), jnp.float32) ** block_levels(splits[15], (D * FF,), ((0, 32),), -0.2, 0.2)), 0.98304, 16.384),
        "second_down": jnp.clip(jnp.exp(math.log(65.536) - 2.7725887 * jax.random.uniform(splits[16], (FF * D,), jnp.float32) ** block_levels(splits[16], (FF * D,), ((0, 32),), -0.2, 0.2)), 4.096, 65.536),
        "second_vec": jnp.clip(jnp.exp(math.log(1048.576) - 2.7725887 * jax.random.uniform(splits[17], (9 * D + FF,), jnp.float32) ** block_levels(splits[17], (9 * D + FF,), ((0, 32),), -0.2, 0.2)), 65.536, 1048.576),
    }


@jax.custom_vjp
def low(v):
    return lax.optimization_barrier(v.astype(jnp.bfloat16)).astype(jnp.float32)

@jax.custom_vjp
def low_back(v):
    return v

def low_keep(v):
    return (low(v), None)

def low_pass(kept, grad):
    return (grad,)

def back_keep(v):
    return (v, None)

def back_low(kept, grad):
    return (low(grad),)
low.defvjp(low_keep, low_pass)
low_back.defvjp(back_keep, back_low)
norm_eps = 1e-05
beta_first = 0.9
beta_second = 0.999
learn_rate = 0.05
vector_rate = 0.3
weight_decay = 0.1
adam_eps = 1e-08
masked_value = -1e+30
rotary_base = 10000.0

def product(left, right):
    return jnp.dot(left, right, precision=lax.Precision.HIGHEST)

def layer_norm(inputs, gain, shift):
    average = lax.optimization_barrier(jnp.mean(inputs, axis=-1, keepdims=True))
    centred = inputs - average
    spread = lax.optimization_barrier(jnp.mean(centred * centred, axis=-1, keepdims=True))
    return centred * lax.rsqrt(spread + norm_eps) * gain + shift

def packing(lengths):
    seq_ends = jnp.cumsum(lengths).astype(jnp.int32)
    row_ids = jnp.arange(TOK_DEV, dtype=jnp.int32)
    passed = row_ids[:, None] >= seq_ends[None, :]
    document = lax.optimization_barrier(jnp.sum(passed.astype(jnp.int32), axis=1)).astype(jnp.int32)
    begins = lax.optimization_barrier(jnp.max(jnp.where(passed, seq_ends[None, :], 0), axis=1)).astype(jnp.int32)
    position = row_ids - begins
    live_rows = row_ids < seq_ends[-1]
    return (document, position, live_rows)

def angles_of(position):
    half_rot = ROT // 2
    inverse = rotary_base ** (-(2.0 * jnp.arange(half_rot, dtype=jnp.float32)) / ROT)
    phases = position.astype(jnp.float32)[..., None] * inverse
    phases = jnp.concatenate([phases, phases], axis=-1)
    return (jnp.cos(phases), jnp.sin(phases))

def rotate(inputs, cosines, sines):
    half_rot = ROT // 2
    turned = inputs[..., :ROT]
    swapped = jnp.concatenate([-turned[..., half_rot:], turned[..., :half_rot]], axis=-1)
    turned = turned * cosines[..., None, :] + swapped * sines[..., None, :]
    return jnp.concatenate([turned, inputs[..., ROT:]], axis=-1)

def attention(queries, key_rows, values, document):
    scaling = HEAD ** (-0.5)
    raw = jnp.einsum('qhd,khd->hqk', queries, key_rows, precision=lax.Precision.HIGHEST) * scaling
    scores = low_back(raw)
    row_ids = jnp.arange(TOK_DEV, dtype=jnp.int32)
    allowed = (document[:, None] == document[None, :]) & (row_ids[None, :] <= row_ids[:, None])
    scores = jnp.where(allowed[None], scores, masked_value)
    probs = low(jax.nn.softmax(scores, axis=-1))
    return jnp.einsum('hqk,khd->qhd', probs, values, precision=lax.Precision.HIGHEST)

def attend_group(items):
    return attention(items[0], items[1], items[2], items[3])

def forward(params, inputs, cosines, sines, document):
    weight_qkv, weight_out, weight_up, weight_down, packed = [low(item) for item in params]
    gain_one = packed[0:D]
    gain_two = packed[D:2 * D]
    shift_one = packed[2 * D:3 * D]
    shift_two = packed[3 * D:4 * D]
    bias_qkv = packed[4 * D:7 * D]
    bias_out = packed[7 * D:8 * D]
    bias_up = packed[8 * D:8 * D + FF]
    bias_down = packed[8 * D + FF:]
    normed_one = low(layer_norm(inputs, gain_one, shift_one))
    normed_two = low(layer_norm(inputs, gain_two, shift_two))
    projected = low_back(product(normed_one, weight_qkv.reshape(D, 3 * D)) + bias_qkv)
    projected = projected.reshape(SHARDS, TOK_DEV, HEADS, 3 * HEAD)
    queries = low(rotate(projected[..., :HEAD], cosines, sines))
    key_rows = low(rotate(projected[..., HEAD:2 * HEAD], cosines, sines))
    values = low(projected[..., 2 * HEAD:])
    context = lax.map(jax.checkpoint(attend_group), (queries, key_rows, values, document))
    context = low(low_back(context.reshape(TOKENS, D)))
    attended = product(context, weight_out.reshape(D, D)) + bias_out
    hidden = low_back(product(normed_two, weight_up.reshape(D, FF)) + bias_up)
    activated = low(jax.nn.gelu(hidden, approximate=False))
    return inputs + attended + product(activated, weight_down.reshape(FF, D)) + bias_down

def adam_step(weight, gradient, moment_one, moment_two, decay_rate, step_rate):
    moment_one = beta_first * moment_one + (1.0 - beta_first) * gradient
    moment_two = beta_second * moment_two + (1.0 - beta_second) * gradient * gradient
    first_hat = moment_one / (1.0 - beta_first ** STEP)
    second_hat = moment_two / (1.0 - beta_second ** STEP)
    weight = weight - step_rate * (first_hat / (jnp.sqrt(second_hat) + adam_eps) + decay_rate * weight)
    return (weight, moment_one, moment_two)

def reference(tokens, cotangent, seq_lens, w_qkv, w_out, w_up, w_down, vectors, first_qkv, first_out, first_up, first_down, first_vec, second_qkv, second_out, second_up, second_down, second_vec):
    document, position, live_rows = jax.vmap(packing)(seq_lens)
    cosines, sines = angles_of(position)
    inputs = tokens.astype(jnp.float32)
    params = (w_qkv, w_out, w_up, w_down, vectors)

    def closed(weights, inputs_f):
        return forward(weights, inputs_f, cosines, sines, document)
    result, pullback = jax.vjp(closed, params, inputs)
    seed_rows = cotangent.astype(jnp.float32) * live_rows.reshape(TOKENS, 1).astype(jnp.float32)
    grads, input_grad = pullback(seed_rows)
    firsts = (first_qkv, first_out, first_up, first_down, first_vec)
    seconds = (second_qkv, second_out, second_up, second_down, second_vec)
    decays = (weight_decay, weight_decay, weight_decay, weight_decay, 0.0)
    rates = (learn_rate, learn_rate, learn_rate, learn_rate, vector_rate)
    updated = [adam_step(weight, gradient, moment_one, moment_two, decay_rate, step_rate) for weight, gradient, moment_one, moment_two, decay_rate, step_rate in zip(params, grads, firsts, seconds, decays, rates)]
    return (result.astype(jnp.bfloat16), input_grad, updated[0][0], updated[1][0], updated[2][0], updated[3][0], updated[4][0], updated[0][1], updated[1][1], updated[2][1], updated[3][1], updated[4][1], updated[0][2], updated[1][2], updated[2][2], updated[3][2], updated[4][2])
```

```python
import jax
import jax.numpy as jnp
from jax import lax
from jax.experimental import pallas as pl
from jax.experimental.pallas import tpu as pltpu
from jax.sharding import PartitionSpec as P

D = 768
HEADS = 12
HEAD = 64
ROT = 16
FF = 3072
TOK_DEV = 1024
BLOCK = 256
PAIR = 2 * HEAD
TRIPLE = 6 * HEAD
STEP = 10


norm_eps = 1e-05
beta_first = 0.9
beta_second = 0.999
learn_rate = 0.05
vector_rate = 0.3
weight_decay = 0.1
adam_eps = 1e-08
masked_value = -1e30
rotary_base = 10000.0


def norm_parts(inputs, gain, shift):
    average = jnp.mean(inputs, axis=-1, keepdims=True)
    centred = inputs - average
    spread = jnp.mean(centred * centred, axis=-1, keepdims=True)
    scaled = lax.rsqrt(spread + norm_eps)
    normal = centred * scaled
    return (normal * gain + shift, normal, scaled)


def norm_back(upstream, normal, scaled, gain):
    weighted = upstream * gain
    inner = weighted - jnp.mean(weighted, axis=-1, keepdims=True)
    inner = inner - normal * jnp.mean(weighted * normal, axis=-1, keepdims=True)
    return (scaled * inner, jnp.sum(upstream * normal, axis=0), jnp.sum(upstream, axis=0))


def packing(lengths):
    seq_ends = jnp.cumsum(lengths)
    row_ids = jnp.arange(TOK_DEV, dtype=jnp.int32)
    passed = row_ids[:, None] >= seq_ends[None, :]
    document = jnp.sum(passed.astype(jnp.int32), axis=1)
    begins = jnp.max(jnp.where(passed, seq_ends[None, :], 0), axis=1)
    return (document, row_ids - begins, row_ids < seq_ends[-1])


def lane_tables(position):
    half_rot = ROT // 2
    inverse = rotary_base ** (-(2.0 * jnp.arange(half_rot, dtype=jnp.float32)) / ROT)
    phases = position.astype(jnp.float32)[:, None] * inverse
    cosines = jnp.cos(phases)
    sines = jnp.sin(phases)
    ones = jnp.ones((TOK_DEV, HEAD - ROT), jnp.float32)
    blank = jnp.zeros((TOK_DEV, HEAD - ROT), jnp.float32)
    gap = jnp.zeros_like(sines)
    keep = jnp.concatenate([cosines, cosines, ones], axis=-1)
    low = jnp.concatenate([-sines, gap, blank], axis=-1)
    high = jnp.concatenate([gap, sines, blank], axis=-1)
    plain = jnp.ones((TOK_DEV, HEAD), jnp.float32)
    empty = jnp.zeros((TOK_DEV, HEAD), jnp.float32)
    return (
        jnp.concatenate([keep, keep, plain] * 2, axis=-1),
        jnp.concatenate([low, low, empty] * 2, axis=-1),
        jnp.concatenate([high, high, empty] * 2, axis=-1),
    )


def dot_nt(left, right):
    return lax.dot_general(
        left, right, (((1,), (1,)), ((), ())), preferred_element_type=jnp.float32
    )


def dot_nn(left, right):
    return lax.dot_general(
        left, right, (((1,), (0,)), ((), ())), preferred_element_type=jnp.float32
    )


def attention_kernel(
    begins_ref,
    normed_ref,
    seed_ref,
    weight_ref,
    bias_ref,
    out_ref,
    keep_ref,
    low_ref,
    high_ref,
    context_ref,
    grad_ref,
    total_ref,
):
    projected = dot_nn(normed_ref[...], weight_ref[...]) + bias_ref[...]
    turned = (
        projected * keep_ref[...]
        + pltpu.roll(projected, TRIPLE - ROT // 2, 1) * low_ref[...]
        + pltpu.roll(projected, ROT // 2, 1) * high_ref[...]
    ).astype(jnp.bfloat16)
    upstream = dot_nt(seed_ref[...], out_ref[...]).astype(jnp.bfloat16)
    scaling = HEAD ** (-0.5)
    heads = []
    for head in range(2):
        at = head * 3 * HEAD
        queries = turned[:, at : at + HEAD] * jnp.bfloat16(scaling)
        keys = turned[:, at + HEAD : at + 2 * HEAD]
        values = turned[:, at + 2 * HEAD : at + 3 * HEAD]
        heads.append(
            (queries, keys, values, upstream[:, head * HEAD : (head + 1) * HEAD], keys.T, values.T)
        )
    total_ref[...] = jnp.zeros_like(total_ref)
    for step in range(TOK_DEV // BLOCK):
        first, last = step * BLOCK, (step + 1) * BLOCK
        begins = begins_ref[:, first:last]
        key_ids = lax.broadcasted_iota(jnp.int32, (last, BLOCK), 0)
        query_ids = first + lax.broadcasted_iota(jnp.int32, (last, BLOCK), 1)
        allowed = (key_ids >= begins) & (key_ids <= query_ids)
        contexts = []
        for head in range(2):
            at = head * 3 * HEAD
            queries, keys, values, above, keys_t, values_t = heads[head]
            query_rows = queries[first:last]
            above_rows = above[first:last]
            scores = jnp.where(allowed, dot_nt(keys[:last], query_rows), masked_value)
            highest = jnp.max(scores, axis=0, keepdims=True)
            expanded = jnp.exp(scores - highest)
            inverse = 1.0 / jnp.sum(expanded, axis=0, keepdims=True)
            probs = expanded * inverse
            probs_low = probs.astype(jnp.bfloat16)
            contexts.append(dot_nn(values_t[:, :last], probs_low))
            dprob = dot_nt(values[:last], above_rows)
            inner = jnp.sum(probs * dprob, axis=0, keepdims=True)
            grad_scores = (probs * (dprob - inner)).astype(jnp.bfloat16)
            grad_queries = dot_nn(keys_t[:, :last], grad_scores) * scaling
            total_ref[first:last, at : at + HEAD] = grad_queries.T
            total_ref[:last, at + HEAD : at + 2 * HEAD] += dot_nn(grad_scores, query_rows)
            total_ref[:last, at + 2 * HEAD : at + 3 * HEAD] += dot_nn(probs_low, above_rows)
        context_ref[first:last, :] = jnp.concatenate(contexts, axis=0).T.astype(jnp.bfloat16)
    total = total_ref[...]
    grad_ref[...] = (
        total * keep_ref[...]
        - pltpu.roll(total, TRIPLE - ROT // 2, 1) * low_ref[...]
        - pltpu.roll(total, ROT // 2, 1) * high_ref[...]
    ).astype(jnp.bfloat16)


def attention(begins, normed, seed_rows, weight_qkv, bias_qkv, weight_out, tables):
    whole = lambda rows, columns: pl.BlockSpec((rows, columns), lambda j: (0, 0))
    pairs = HEADS // 2
    return pl.pallas_call(
        attention_kernel,
        grid=(pairs,),
        in_specs=[
            whole(1, TOK_DEV),
            whole(TOK_DEV, D),
            whole(TOK_DEV, D),
            pl.BlockSpec((D, TRIPLE), lambda j: (0, j)),
            pl.BlockSpec((1, TRIPLE), lambda j: (0, j)),
            pl.BlockSpec((PAIR, D), lambda j: (j, 0)),
            whole(TOK_DEV, TRIPLE),
            whole(TOK_DEV, TRIPLE),
            whole(TOK_DEV, TRIPLE),
        ],
        out_specs=[
            pl.BlockSpec((TOK_DEV, PAIR), lambda j: (0, j)),
            pl.BlockSpec((TOK_DEV, TRIPLE), lambda j: (0, j)),
        ],
        out_shape=[
            jax.ShapeDtypeStruct((TOK_DEV, D), jnp.bfloat16),
            jax.ShapeDtypeStruct((TOK_DEV, 3 * D), jnp.bfloat16),
        ],
        scratch_shapes=[pltpu.VMEM((TOK_DEV, TRIPLE), jnp.float32)],
        compiler_params=pltpu.CompilerParams(vmem_limit_bytes=52 * 2**20),
        cost_estimate=pl.CostEstimate(
            flops=16_000_000_000, bytes_accessed=20_000_000, transcendentals=8_000_000
        ),
    )(begins, normed, seed_rows, weight_qkv, bias_qkv, weight_out, *tables)


def adam_step(weight, gradient, moment_one, moment_two, decay_rate, step_rate):
    moment_one = beta_first * moment_one + (1.0 - beta_first) * gradient
    moment_two = beta_second * moment_two + (1.0 - beta_second) * gradient * gradient
    first_hat = moment_one / (1.0 - beta_first**STEP)
    second_hat = moment_two / (1.0 - beta_second**STEP)
    weight = weight - step_rate * (
        first_hat / (jnp.sqrt(second_hat) + adam_eps) + decay_rate * weight
    )
    return (weight, moment_one, moment_two)


def per_device(
    tokens,
    cotangent,
    seq_lens,
    w_qkv,
    w_out,
    w_up,
    w_down,
    vectors,
    first_qkv,
    first_out,
    first_up,
    first_down,
    first_vec,
    second_qkv,
    second_out,
    second_up,
    second_down,
    second_vec,
):
    axes = ("dp", "group")
    shards = D // (w_out.shape[0] // D)

    def gather(shard, rows):
        low = shard.astype(jnp.bfloat16).reshape(rows // shards, -1)
        return lax.all_gather(low, axes, axis=0, tiled=True)

    weight_qkv = gather(w_qkv, D)
    weight_out = gather(w_out, D)
    weight_up = gather(w_up, D)
    weight_down = gather(w_down, FF)
    packed = lax.all_gather(vectors.astype(jnp.bfloat16), axes, axis=0, tiled=True).astype(jnp.float32)
    gain_one = packed[0:D]
    gain_two = packed[D : 2 * D]
    shift_one = packed[2 * D : 3 * D]
    shift_two = packed[3 * D : 4 * D]
    bias_qkv = packed[4 * D : 7 * D]
    bias_out = packed[7 * D : 8 * D]
    bias_up = packed[8 * D : 8 * D + FF]
    bias_down = packed[8 * D + FF :]
    document, position, live_rows = packing(seq_lens[0])
    inputs = tokens.astype(jnp.float32)
    normed_one, normal_one, scaled_one = norm_parts(inputs, gain_one, shift_one)
    normed_two, normal_two, scaled_two = norm_parts(inputs, gain_two, shift_two)
    normed_one = normed_one.astype(jnp.bfloat16)
    normed_two = normed_two.astype(jnp.bfloat16)
    seed_rows = jnp.where(live_rows[:, None], cotangent, jnp.zeros_like(cotangent))
    begins = jnp.arange(TOK_DEV, dtype=jnp.int32) - position
    context, grad_projected = attention(
        begins[None, :],
        normed_one,
        seed_rows,
        weight_qkv,
        bias_qkv[None, :],
        weight_out,
        lane_tables(position),
    )
    attended = jnp.dot(context, weight_out, preferred_element_type=jnp.float32) + bias_out
    hidden = jnp.dot(normed_two, weight_up, preferred_element_type=jnp.float32) + bias_up
    activation, gelu_back = jax.vjp(lambda entry: jax.nn.gelu(entry, approximate=False), hidden)
    activated = activation.astype(jnp.bfloat16)
    result = (
        inputs
        + attended
        + jnp.dot(activated, weight_down, preferred_element_type=jnp.float32)
        + bias_down
    )
    seed_float = seed_rows.astype(jnp.float32)
    grad_down = jnp.einsum("tf,td->fd", activated, seed_rows, preferred_element_type=jnp.float32)
    grad_out = jnp.einsum("tc,td->cd", context, seed_rows, preferred_element_type=jnp.float32)
    grad_act = jnp.einsum("td,fd->tf", seed_rows, weight_down, preferred_element_type=jnp.float32)
    grad_hidden = gelu_back(grad_act)[0].astype(jnp.bfloat16)
    grad_up = jnp.einsum("td,tf->df", normed_two, grad_hidden, preferred_element_type=jnp.float32)
    grad_two = jnp.einsum("tf,df->td", grad_hidden, weight_up, preferred_element_type=jnp.float32)
    grad_qkv = jnp.einsum(
        "td,te->de", normed_one, grad_projected, preferred_element_type=jnp.float32
    )
    grad_one = jnp.einsum(
        "te,de->td", grad_projected, weight_qkv, preferred_element_type=jnp.float32
    )
    input_one, gain_grad_one, shift_grad_one = norm_back(grad_one, normal_one, scaled_one, gain_one)
    input_two, gain_grad_two, shift_grad_two = norm_back(grad_two, normal_two, scaled_two, gain_two)
    input_grad = seed_float + input_one + input_two
    seed_total = jnp.sum(seed_float, axis=0)
    grad_vec = jnp.concatenate(
        [
            gain_grad_one,
            gain_grad_two,
            shift_grad_one,
            shift_grad_two,
            jnp.sum(grad_projected.astype(jnp.float32), axis=0),
            seed_total,
            jnp.sum(grad_hidden.astype(jnp.float32), axis=0),
            seed_total,
        ]
    )
    def scatter(gradient):
        low = gradient.astype(jnp.bfloat16)
        part = lax.psum_scatter(low, axes, scatter_dimension=0, tiled=True)
        return part.astype(jnp.float32).reshape(-1)

    summed = (
        scatter(grad_qkv),
        scatter(grad_out),
        scatter(grad_up),
        scatter(grad_down),
        lax.psum_scatter(grad_vec, axes, scatter_dimension=0, tiled=True),
    )
    masters = (w_qkv, w_out, w_up, w_down, vectors)
    firsts = (first_qkv, first_out, first_up, first_down, first_vec)
    seconds = (second_qkv, second_out, second_up, second_down, second_vec)
    decays = (weight_decay, weight_decay, weight_decay, weight_decay, 0.0)
    rates = (learn_rate, learn_rate, learn_rate, learn_rate, vector_rate)
    updated = [
        adam_step(weight, gradient, moment_one, moment_two, decay_rate, step_rate)
        for weight, gradient, moment_one, moment_two, decay_rate, step_rate in zip(
            masters, summed, firsts, seconds, decays, rates
        )
    ]
    return (
        result.astype(jnp.bfloat16),
        input_grad,
        updated[0][0],
        updated[1][0],
        updated[2][0],
        updated[3][0],
        updated[4][0],
        updated[0][1],
        updated[1][1],
        updated[2][1],
        updated[3][1],
        updated[4][1],
        updated[0][2],
        updated[1][2],
        updated[2][2],
        updated[3][2],
        updated[4][2],
    )


def solution(mesh):
    placed = (
        P(("dp", "group"), None),
        P(("dp", "group"), None),
        P(("dp", "group"), None),
        P(("dp", "group")),
        P(("dp", "group")),
        P(("dp", "group")),
        P(("dp", "group")),
        P(("dp", "group")),
        P(("dp", "group")),
        P(("dp", "group")),
        P(("dp", "group")),
        P(("dp", "group")),
        P(("dp", "group")),
        P(("dp", "group")),
        P(("dp", "group")),
        P(("dp", "group")),
        P(("dp", "group")),
        P(("dp", "group")),
    )
    return jax.shard_map(
        per_device,
        mesh=mesh,
        in_specs=placed,
        out_specs=(
            P(("dp", "group"), None),
            P(("dp", "group"), None),
            P(("dp", "group")),
            P(("dp", "group")),
            P(("dp", "group")),
            P(("dp", "group")),
            P(("dp", "group")),
            P(("dp", "group")),
            P(("dp", "group")),
            P(("dp", "group")),
            P(("dp", "group")),
            P(("dp", "group")),
            P(("dp", "group")),
            P(("dp", "group")),
            P(("dp", "group")),
            P(("dp", "group")),
            P(("dp", "group")),
        ),
        check_vma=False,
    )
```

```python
import functools

import jax
import jax.numpy as jnp
from jax import lax
from jax.experimental import pallas as pl
from jax.experimental.pallas import tpu as pltpu
from jax.sharding import PartitionSpec as P

D = 768
HEADS = 12
HEAD = 64
ROT = 16
FF = 3072
TOK_DEV = 1024
BLOCK = 256
PAIR = 2 * HEAD
TRIPLE = 6 * HEAD
STEP = 10


norm_eps = 1e-05
beta_first = 0.9
beta_second = 0.999
learn_rate = 0.05
vector_rate = 0.3
weight_decay = 0.1
adam_eps = 1e-08
masked_value = -1e30
rotary_base = 10000.0


def norm_parts(inputs, gain, shift):
    average = jnp.mean(inputs, axis=-1, keepdims=True)
    centred = inputs - average
    spread = jnp.mean(centred * centred, axis=-1, keepdims=True)
    scaled = lax.rsqrt(spread + norm_eps)
    normal = centred * scaled
    return (normal * gain + shift, normal, scaled)


def norm_back(upstream, normal, scaled, gain):
    weighted = upstream * gain
    inner = weighted - jnp.mean(weighted, axis=-1, keepdims=True)
    inner = inner - normal * jnp.mean(weighted * normal, axis=-1, keepdims=True)
    return (scaled * inner, jnp.sum(upstream * normal, axis=0), jnp.sum(upstream, axis=0))


def packing(lengths):
    seq_ends = jnp.cumsum(lengths)
    row_ids = jnp.arange(TOK_DEV, dtype=jnp.int32)
    passed = row_ids[:, None] >= seq_ends[None, :]
    document = jnp.sum(passed.astype(jnp.int32), axis=1)
    begins = jnp.max(jnp.where(passed, seq_ends[None, :], 0), axis=1)
    return (document, row_ids - begins, row_ids < seq_ends[-1])


def lane_tables(position):
    half_rot = ROT // 2
    inverse = rotary_base ** (-(2.0 * jnp.arange(half_rot, dtype=jnp.float32)) / ROT)
    phases = position.astype(jnp.float32)[:, None] * inverse
    cosines = jnp.cos(phases)
    sines = jnp.sin(phases)
    ones = jnp.ones((TOK_DEV, HEAD - ROT), jnp.float32)
    blank = jnp.zeros((TOK_DEV, HEAD - ROT), jnp.float32)
    gap = jnp.zeros_like(sines)
    return (
        jnp.concatenate([cosines, cosines, ones] * 2, axis=-1),
        jnp.concatenate([-sines, gap, blank] * 2, axis=-1),
        jnp.concatenate([gap, sines, blank] * 2, axis=-1),
    )


def widen(narrow, plain):
    lane = lax.broadcasted_iota(jnp.int32, narrow.shape, 1)
    upper = jnp.where(lane >= HEAD, narrow, plain)
    lower = jnp.where(lane < HEAD, narrow, plain)
    return jnp.concatenate([narrow, upper, lower], axis=1)


def dot_nt(left, right):
    return lax.dot_general(
        left, right, (((1,), (1,)), ((), ())), preferred_element_type=jnp.float32
    )


def dot_nn(left, right):
    return lax.dot_general(
        left, right, (((1,), (0,)), ((), ())), preferred_element_type=jnp.float32
    )


def attention_kernel(
    begins_ref,
    normed_ref,
    seed_ref,
    weight_ref,
    bias_ref,
    out_ref,
    cosines_ref,
    low_sines_ref,
    high_sines_ref,
    context_ref,
    grad_ref,
    total_ref,
    keep_ref,
    low_ref,
    high_ref,
):
    @pl.when(pl.program_id(0) == 0)
    def _():
        keep_ref[...] = widen(cosines_ref[...], 1.0)
        low_ref[...] = widen(low_sines_ref[...], 0.0)
        high_ref[...] = widen(high_sines_ref[...], 0.0)

    projected = dot_nn(normed_ref[...], weight_ref[...]) + bias_ref[...]
    turned = (
        projected * keep_ref[...]
        + pltpu.roll(projected, TRIPLE - ROT // 2, 1) * low_ref[...]
        + pltpu.roll(projected, ROT // 2, 1) * high_ref[...]
    ).astype(jnp.bfloat16)
    upstream = dot_nt(seed_ref[...], out_ref[...]).astype(jnp.bfloat16)
    scaling = HEAD ** (-0.5)
    heads = []
    for head in range(2):
        at = head * 3 * HEAD
        queries = turned[:, at : at + HEAD] * jnp.bfloat16(scaling)
        keys = turned[:, at + HEAD : at + 2 * HEAD]
        values = turned[:, at + 2 * HEAD : at + 3 * HEAD]
        heads.append(
            (queries, keys, values, upstream[:, head * HEAD : (head + 1) * HEAD], keys.T, values.T)
        )
    total_ref[...] = jnp.zeros_like(total_ref)
    for step in range(TOK_DEV // BLOCK):
        first, last = step * BLOCK, (step + 1) * BLOCK
        begins = begins_ref[:, first:last]
        key_ids = lax.broadcasted_iota(jnp.int32, (last, BLOCK), 0)
        query_ids = first + lax.broadcasted_iota(jnp.int32, (last, BLOCK), 1)
        allowed = (key_ids >= begins) & (key_ids <= query_ids)
        contexts = []
        for head in range(2):
            at = head * 3 * HEAD
            queries, keys, values, above, keys_t, values_t = heads[head]
            query_rows = queries[first:last]
            above_rows = above[first:last]
            scores = jnp.where(allowed, dot_nt(keys[:last], query_rows), masked_value)
            highest = jnp.max(scores, axis=0, keepdims=True)
            expanded = jnp.exp(scores - highest)
            inverse = 1.0 / jnp.sum(expanded, axis=0, keepdims=True)
            probs = expanded * inverse
            probs_low = probs.astype(jnp.bfloat16)
            contexts.append(dot_nn(values_t[:, :last], probs_low))
            dprob = dot_nt(values[:last], above_rows)
            inner = jnp.sum(probs * dprob, axis=0, keepdims=True)
            grad_scores = (probs * (dprob - inner)).astype(jnp.bfloat16)
            grad_queries = dot_nn(keys_t[:, :last], grad_scores) * scaling
            total_ref[first:last, at : at + HEAD] = grad_queries.T
            total_ref[:last, at + HEAD : at + 2 * HEAD] += dot_nn(grad_scores, query_rows)
            total_ref[:last, at + 2 * HEAD : at + 3 * HEAD] += dot_nn(probs_low, above_rows)
        context_ref[first:last, :] = jnp.concatenate(contexts, axis=0).T.astype(jnp.bfloat16)
    total = total_ref[...]
    grad_ref[...] = (
        total * keep_ref[...]
        - pltpu.roll(total, TRIPLE - ROT // 2, 1) * low_ref[...]
        - pltpu.roll(total, ROT // 2, 1) * high_ref[...]
    ).astype(jnp.bfloat16)


def attention(begins, normed, seed_rows, weight_qkv, bias_qkv, weight_out, tables):
    whole = lambda rows, columns: pl.BlockSpec((rows, columns), lambda j: (0, 0))
    pairs = HEADS // 2
    return pl.pallas_call(
        attention_kernel,
        grid=(pairs,),
        in_specs=[
            whole(1, TOK_DEV),
            whole(TOK_DEV, D),
            whole(TOK_DEV, D),
            pl.BlockSpec((D, TRIPLE), lambda j: (0, j)),
            pl.BlockSpec((1, TRIPLE), lambda j: (0, j)),
            pl.BlockSpec((PAIR, D), lambda j: (j, 0)),
            whole(TOK_DEV, PAIR),
            whole(TOK_DEV, PAIR),
            whole(TOK_DEV, PAIR),
        ],
        out_specs=[
            pl.BlockSpec((TOK_DEV, PAIR), lambda j: (0, j)),
            pl.BlockSpec((TOK_DEV, TRIPLE), lambda j: (0, j)),
        ],
        out_shape=[
            jax.ShapeDtypeStruct((TOK_DEV, D), jnp.bfloat16),
            jax.ShapeDtypeStruct((TOK_DEV, 3 * D), jnp.bfloat16),
        ],
        scratch_shapes=[pltpu.VMEM((TOK_DEV, TRIPLE), jnp.float32)] * 4,
        compiler_params=pltpu.CompilerParams(vmem_limit_bytes=52 * 2**20),
        cost_estimate=pl.CostEstimate(
            flops=16_000_000_000, bytes_accessed=20_000_000, transcendentals=8_000_000
        ),
    )(begins, normed, seed_rows, weight_qkv, bias_qkv, weight_out, *tables)


def exchange(block, bit, devices):
    pairs = [(index, index ^ (1 << bit)) for index in range(devices)]
    return lax.ppermute(block, ("dp", "group"), pairs)


def own_bit(bit, group_size):
    index = lax.axis_index("dp") * group_size + lax.axis_index("group")
    return lax.rem(lax.div(index, 1 << bit), 2)


def bit_order(devices, group_size, flipped):
    group_bits = group_size.bit_length() - 1
    total_bits = devices.bit_length() - 1
    chips = list(range(group_bits + 1, total_bits))
    if flipped:
        chips = chips[::-1]
    return [group_bits] + chips + list(range(group_bits))[::-1]


def sum_scatter(block, devices, group_size, flipped):
    left = list(range(devices.bit_length() - 1))[::-1]
    columns = block.shape[1]
    for bit in bit_order(devices, group_size, flipped):
        before = 2 ** left.index(bit)
        view = block.reshape(before, 2, -1, columns)
        own = own_bit(bit, group_size)
        kept = lax.dynamic_index_in_dim(view, own, 1, keepdims=False)
        sent = lax.dynamic_index_in_dim(view, 1 - own, 1, keepdims=False)
        left.remove(bit)
        arrived = exchange(sent, bit, devices)
        block = kept.astype(jnp.float32) + arrived.astype(jnp.float32)
        if left:
            block = block.astype(jnp.bfloat16)
        block = block.reshape(-1, columns)
    return block


def gather_rows(block, devices, group_size, flipped):
    held = []
    columns = block.shape[1]
    for bit in bit_order(devices, group_size, flipped)[::-1]:
        arrived = exchange(block, bit, devices)
        held = sorted(held + [bit], reverse=True)
        before = 2 ** held.index(bit)
        first = own_bit(bit, group_size) == 0
        low = jnp.where(first, block, arrived).reshape(before, -1, columns)
        high = jnp.where(first, arrived, block).reshape(before, -1, columns)
        block = jnp.stack([low, high], axis=1).reshape(-1, columns)
    return block


def adam_step(weight, gradient, moment_one, moment_two, decay_rate, step_rate):
    moment_one = beta_first * moment_one + (1.0 - beta_first) * gradient
    moment_two = beta_second * moment_two + (1.0 - beta_second) * gradient * gradient
    first_hat = moment_one / (1.0 - beta_first**STEP)
    second_hat = moment_two / (1.0 - beta_second**STEP)
    weight = weight - step_rate * (
        first_hat / (jnp.sqrt(second_hat) + adam_eps) + decay_rate * weight
    )
    return (weight, moment_one, moment_two)


def per_device(
    devices,
    group_size,
    tokens,
    cotangent,
    seq_lens,
    w_qkv,
    w_out,
    w_up,
    w_down,
    vectors,
    first_qkv,
    first_out,
    first_up,
    first_down,
    first_vec,
    second_qkv,
    second_out,
    second_up,
    second_down,
    second_vec,
):
    shard_rows = w_out.shape[0] // D
    low_qkv = w_qkv.astype(jnp.bfloat16).reshape(shard_rows, 3 * D)
    low_out = w_out.astype(jnp.bfloat16).reshape(shard_rows, D)
    low_up = w_up.astype(jnp.bfloat16).reshape(shard_rows, FF)
    low_down = w_down.astype(jnp.bfloat16).reshape(-1, D)
    low_vec = vectors.astype(jnp.bfloat16).reshape(shard_rows, -1)
    vec_width = low_vec.shape[1]
    vec_pad = ((0, 0), (0, 128 - vec_width))
    low_up = jnp.concatenate([low_up, jnp.pad(low_vec, vec_pad)], axis=1)
    low_late = jnp.concatenate([low_qkv[:, 2 * D :], low_out], axis=1)
    full_up = gather_rows(low_up, devices, group_size, False)
    weight_down = gather_rows(low_down, devices, group_size, True)
    full_early = gather_rows(low_qkv[:, : 2 * D], devices, group_size, False)
    full_late = gather_rows(low_late, devices, group_size, True)
    weight_up = full_up[:, :FF]
    packed = full_up[:, FF : FF + vec_width].reshape(-1).astype(jnp.float32)
    weight_qkv = jnp.concatenate([full_early, full_late[:, :D]], axis=1)
    weight_out = full_late[:, D:]
    gain_one = packed[0:D]
    gain_two = packed[D : 2 * D]
    shift_one = packed[2 * D : 3 * D]
    shift_two = packed[3 * D : 4 * D]
    bias_qkv = packed[4 * D : 7 * D]
    bias_out = packed[7 * D : 8 * D]
    bias_up = packed[8 * D : 8 * D + FF]
    bias_down = packed[8 * D + FF :]
    document, position, live_rows = packing(seq_lens[0])
    inputs = tokens.astype(jnp.float32)
    normed_one, normal_one, scaled_one = norm_parts(inputs, gain_one, shift_one)
    normed_two, normal_two, scaled_two = norm_parts(inputs, gain_two, shift_two)
    normed_one = normed_one.astype(jnp.bfloat16)
    normed_two = normed_two.astype(jnp.bfloat16)
    seed_rows = jnp.where(live_rows[:, None], cotangent, jnp.zeros_like(cotangent))
    begins = jnp.arange(TOK_DEV, dtype=jnp.int32) - position
    context, grad_projected = attention(
        begins[None, :],
        normed_one,
        seed_rows,
        weight_qkv,
        bias_qkv[None, :],
        weight_out,
        lane_tables(position),
    )
    attended = jnp.dot(context, weight_out, preferred_element_type=jnp.float32) + bias_out
    hidden = jnp.dot(normed_two, weight_up, preferred_element_type=jnp.float32) + bias_up
    activation, gelu_back = jax.vjp(lambda entry: jax.nn.gelu(entry, approximate=False), hidden)
    activated = activation.astype(jnp.bfloat16)
    result = (
        inputs
        + attended
        + jnp.dot(activated, weight_down, preferred_element_type=jnp.float32)
        + bias_down
    )
    seed_float = seed_rows.astype(jnp.float32)
    grad_down = jnp.einsum("tf,td->fd", activated, seed_rows, preferred_element_type=jnp.float32)
    grad_out = jnp.einsum("tc,td->cd", context, seed_rows, preferred_element_type=jnp.float32)
    grad_act = jnp.einsum("td,fd->tf", seed_rows, weight_down, preferred_element_type=jnp.float32)
    grad_hidden = gelu_back(grad_act)[0].astype(jnp.bfloat16)
    grad_up = jnp.einsum("td,tf->df", normed_two, grad_hidden, preferred_element_type=jnp.float32)
    grad_two = jnp.einsum("tf,df->td", grad_hidden, weight_up, preferred_element_type=jnp.float32)
    grad_qkv = jnp.einsum(
        "td,te->de", normed_one, grad_projected, preferred_element_type=jnp.float32
    )
    grad_one = jnp.einsum(
        "te,de->td", grad_projected, weight_qkv, preferred_element_type=jnp.float32
    )
    input_one, gain_grad_one, shift_grad_one = norm_back(grad_one, normal_one, scaled_one, gain_one)
    input_two, gain_grad_two, shift_grad_two = norm_back(grad_two, normal_two, scaled_two, gain_two)
    input_grad = seed_float + input_one + input_two
    seed_total = jnp.sum(seed_float, axis=0)
    grad_vec = jnp.concatenate(
        [
            gain_grad_one,
            gain_grad_two,
            shift_grad_one,
            shift_grad_two,
            jnp.sum(grad_projected.astype(jnp.float32), axis=0),
            seed_total,
            jnp.sum(grad_hidden.astype(jnp.float32), axis=0),
            seed_total,
        ]
    )
    grad_early = grad_qkv[:, : 2 * D].astype(jnp.bfloat16)
    grad_late = jnp.concatenate(
        [
            grad_qkv[:, 2 * D :].astype(jnp.bfloat16),
            grad_out.astype(jnp.bfloat16),
            jnp.pad(grad_vec.reshape(D, -1), vec_pad).astype(jnp.bfloat16),
        ],
        axis=1,
    )
    sum_up = sum_scatter(grad_up.astype(jnp.bfloat16), devices, group_size, False)
    sum_down = sum_scatter(grad_down.astype(jnp.bfloat16), devices, group_size, True)
    sum_early = sum_scatter(grad_early, devices, group_size, False)
    sum_late = sum_scatter(grad_late, devices, group_size, True)
    summed = (
        jnp.concatenate([sum_early, sum_late[:, :D]], axis=1).reshape(-1),
        sum_late[:, D : 2 * D].reshape(-1),
        sum_up.reshape(-1),
        sum_down.reshape(-1),
        sum_late[:, 2 * D : 2 * D + vec_width].reshape(-1),
    )
    masters = (w_qkv, w_out, w_up, w_down, vectors)
    firsts = (first_qkv, first_out, first_up, first_down, first_vec)
    seconds = (second_qkv, second_out, second_up, second_down, second_vec)
    decays = (weight_decay, weight_decay, weight_decay, weight_decay, 0.0)
    rates = (learn_rate, learn_rate, learn_rate, learn_rate, vector_rate)
    updated = [
        adam_step(weight, gradient, moment_one, moment_two, decay_rate, step_rate)
        for weight, gradient, moment_one, moment_two, decay_rate, step_rate in zip(
            masters, summed, firsts, seconds, decays, rates
        )
    ]
    return (
        result.astype(jnp.bfloat16),
        input_grad,
        updated[0][0],
        updated[1][0],
        updated[2][0],
        updated[3][0],
        updated[4][0],
        updated[0][1],
        updated[1][1],
        updated[2][1],
        updated[3][1],
        updated[4][1],
        updated[0][2],
        updated[1][2],
        updated[2][2],
        updated[3][2],
        updated[4][2],
    )


def solution(mesh):
    placed = (
        P(("dp", "group"), None),
        P(("dp", "group"), None),
        P(("dp", "group"), None),
        P(("dp", "group")),
        P(("dp", "group")),
        P(("dp", "group")),
        P(("dp", "group")),
        P(("dp", "group")),
        P(("dp", "group")),
        P(("dp", "group")),
        P(("dp", "group")),
        P(("dp", "group")),
        P(("dp", "group")),
        P(("dp", "group")),
        P(("dp", "group")),
        P(("dp", "group")),
        P(("dp", "group")),
        P(("dp", "group")),
    )
    group_size = mesh.shape["group"]
    devices = mesh.shape["dp"] * group_size
    return jax.shard_map(
        functools.partial(per_device, devices, group_size),
        mesh=mesh,
        in_specs=placed,
        out_specs=(
            P(("dp", "group"), None),
            P(("dp", "group"), None),
            P(("dp", "group")),
            P(("dp", "group")),
            P(("dp", "group")),
            P(("dp", "group")),
            P(("dp", "group")),
            P(("dp", "group")),
            P(("dp", "group")),
            P(("dp", "group")),
            P(("dp", "group")),
            P(("dp", "group")),
            P(("dp", "group")),
            P(("dp", "group")),
            P(("dp", "group")),
            P(("dp", "group")),
            P(("dp", "group")),
        ),
        check_vma=False,
    )
```

```python
import functools

import jax
import jax.numpy as jnp
from jax import lax
from jax.experimental import pallas as pl
from jax.experimental.pallas import tpu as pltpu
from jax.sharding import PartitionSpec as P

D = 768
HEADS = 12
HEAD = 64
ROT = 16
FF = 3072
TOK_DEV = 1024
BLOCK = 256
PAIR = 2 * HEAD
TRIPLE = 6 * HEAD
STEP = 10


norm_eps = 1e-05
beta_first = 0.9
beta_second = 0.999
learn_rate = 0.05
vector_rate = 0.3
weight_decay = 0.1
adam_eps = 1e-08
masked_value = -1e30
rotary_base = 10000.0


def norm_parts(inputs, gain, shift):
    average = jnp.mean(inputs, axis=-1, keepdims=True)
    centred = inputs - average
    spread = jnp.mean(centred * centred, axis=-1, keepdims=True)
    scaled = lax.rsqrt(spread + norm_eps)
    normal = centred * scaled
    return (normal * gain + shift, normal, scaled)


def norm_back(upstream, normal, scaled, gain):
    weighted = upstream * gain
    inner = weighted - jnp.mean(weighted, axis=-1, keepdims=True)
    inner = inner - normal * jnp.mean(weighted * normal, axis=-1, keepdims=True)
    return (scaled * inner, jnp.sum(upstream * normal, axis=0), jnp.sum(upstream, axis=0))


def packing(lengths):
    seq_ends = jnp.cumsum(lengths)
    row_ids = jnp.arange(TOK_DEV, dtype=jnp.int32)
    passed = row_ids[:, None] >= seq_ends[None, :]
    document = jnp.sum(passed.astype(jnp.int32), axis=1)
    begins = jnp.max(jnp.where(passed, seq_ends[None, :], 0), axis=1)
    return (document, row_ids - begins, row_ids < seq_ends[-1])


def lane_tables(position):
    half_rot = ROT // 2
    inverse = rotary_base ** (-(2.0 * jnp.arange(half_rot, dtype=jnp.float32)) / ROT)
    phases = position.astype(jnp.float32)[:, None] * inverse
    cosines = jnp.cos(phases)
    sines = jnp.sin(phases)
    ones = jnp.ones((TOK_DEV, HEAD - ROT), jnp.float32)
    blank = jnp.zeros((TOK_DEV, HEAD - ROT), jnp.float32)
    gap = jnp.zeros_like(sines)
    return (
        jnp.concatenate([cosines, cosines, ones] * 2, axis=-1),
        jnp.concatenate([-sines, gap, blank] * 2, axis=-1),
        jnp.concatenate([gap, sines, blank] * 2, axis=-1),
    )


def widen(narrow, plain):
    lane = lax.broadcasted_iota(jnp.int32, narrow.shape, 1)
    upper = jnp.where(lane >= HEAD, narrow, plain)
    lower = jnp.where(lane < HEAD, narrow, plain)
    return jnp.concatenate([narrow, upper, lower], axis=1)


def dot_nt(left, right):
    return lax.dot_general(
        left, right, (((1,), (1,)), ((), ())), preferred_element_type=jnp.float32
    )


def dot_nn(left, right):
    return lax.dot_general(
        left, right, (((1,), (0,)), ((), ())), preferred_element_type=jnp.float32
    )


def attention_kernel(
    begins_ref,
    normed_ref,
    seed_ref,
    weight_ref,
    bias_ref,
    out_ref,
    cosines_ref,
    low_sines_ref,
    high_sines_ref,
    context_ref,
    grad_ref,
    total_ref,
    keep_ref,
    low_ref,
    high_ref,
):
    @pl.when(pl.program_id(0) == 0)
    def _():
        keep_ref[...] = widen(cosines_ref[...], 1.0)
        low_ref[...] = widen(low_sines_ref[...], 0.0)
        high_ref[...] = widen(high_sines_ref[...], 0.0)

    projected = dot_nn(normed_ref[...], weight_ref[...]) + bias_ref[...]
    turned = (
        projected * keep_ref[...]
        + pltpu.roll(projected, TRIPLE - ROT // 2, 1) * low_ref[...]
        + pltpu.roll(projected, ROT // 2, 1) * high_ref[...]
    ).astype(jnp.bfloat16)
    upstream = dot_nt(seed_ref[...], out_ref[...]).astype(jnp.bfloat16)
    scaling = HEAD ** (-0.5)
    heads = []
    for head in range(2):
        at = head * 3 * HEAD
        queries = turned[:, at : at + HEAD] * jnp.bfloat16(scaling)
        keys = turned[:, at + HEAD : at + 2 * HEAD]
        values = turned[:, at + 2 * HEAD : at + 3 * HEAD]
        heads.append(
            (queries, keys, values, upstream[:, head * HEAD : (head + 1) * HEAD], keys.T, values.T)
        )
    total_ref[...] = jnp.zeros_like(total_ref)
    for step in range(TOK_DEV // BLOCK):
        first, last = step * BLOCK, (step + 1) * BLOCK
        begins = begins_ref[:, first:last]
        key_ids = lax.broadcasted_iota(jnp.int32, (last, BLOCK), 0)
        query_ids = first + lax.broadcasted_iota(jnp.int32, (last, BLOCK), 1)
        allowed = (key_ids >= begins) & (key_ids <= query_ids)
        contexts = []
        for head in range(2):
            at = head * 3 * HEAD
            queries, keys, values, above, keys_t, values_t = heads[head]
            query_rows = queries[first:last]
            above_rows = above[first:last]
            scores = jnp.where(allowed, dot_nt(keys[:last], query_rows), masked_value)
            highest = jnp.max(scores, axis=0, keepdims=True)
            expanded = jnp.exp(scores - highest)
            inverse = 1.0 / jnp.sum(expanded, axis=0, keepdims=True)
            probs = expanded * inverse
            probs_low = probs.astype(jnp.bfloat16)
            contexts.append(dot_nn(values_t[:, :last], probs_low))
            dprob = dot_nt(values[:last], above_rows)
            inner = jnp.sum(probs * dprob, axis=0, keepdims=True)
            grad_scores = (probs * (dprob - inner)).astype(jnp.bfloat16)
            grad_queries = dot_nn(keys_t[:, :last], grad_scores) * scaling
            total_ref[first:last, at : at + HEAD] = grad_queries.T
            total_ref[:last, at + HEAD : at + 2 * HEAD] += dot_nn(grad_scores, query_rows)
            total_ref[:last, at + 2 * HEAD : at + 3 * HEAD] += dot_nn(probs_low, above_rows)
        context_ref[first:last, :] = jnp.concatenate(contexts, axis=0).T.astype(jnp.bfloat16)
    total = total_ref[...]
    grad_ref[...] = (
        total * keep_ref[...]
        - pltpu.roll(total, TRIPLE - ROT // 2, 1) * low_ref[...]
        - pltpu.roll(total, ROT // 2, 1) * high_ref[...]
    ).astype(jnp.bfloat16)


def attention(begins, normed, seed_rows, weight_qkv, bias_qkv, weight_out, tables, first, pairs):
    whole = lambda rows, columns: pl.BlockSpec((rows, columns), lambda j: (0, 0))
    return pl.pallas_call(
        attention_kernel,
        grid=(pairs,),
        in_specs=[
            whole(1, TOK_DEV),
            whole(TOK_DEV, D),
            whole(TOK_DEV, D),
            pl.BlockSpec((D, TRIPLE), lambda j: (0, j + first)),
            pl.BlockSpec((1, TRIPLE), lambda j: (0, j + first)),
            pl.BlockSpec((PAIR, D), lambda j: (j + first, 0)),
            whole(TOK_DEV, PAIR),
            whole(TOK_DEV, PAIR),
            whole(TOK_DEV, PAIR),
        ],
        out_specs=[
            pl.BlockSpec((TOK_DEV, PAIR), lambda j: (0, j)),
            pl.BlockSpec((TOK_DEV, TRIPLE), lambda j: (0, j)),
        ],
        out_shape=[
            jax.ShapeDtypeStruct((TOK_DEV, pairs * PAIR), jnp.bfloat16),
            jax.ShapeDtypeStruct((TOK_DEV, pairs * TRIPLE), jnp.bfloat16),
        ],
        scratch_shapes=[pltpu.VMEM((TOK_DEV, TRIPLE), jnp.float32)] * 4,
        compiler_params=pltpu.CompilerParams(vmem_limit_bytes=52 * 2**20),
        cost_estimate=pl.CostEstimate(
            flops=pairs * 5_000_000_000, bytes_accessed=8_000_000, transcendentals=pairs * 1_400_000
        ),
    )(begins, normed, seed_rows, weight_qkv, bias_qkv, weight_out, *tables)


def exchange(block, bit, devices):
    pairs = [(index, index ^ (1 << bit)) for index in range(devices)]
    return lax.ppermute(block, ("dp", "group"), pairs)


def own_bit(bit, group_size):
    index = lax.axis_index("dp") * group_size + lax.axis_index("group")
    return lax.rem(lax.div(index, 1 << bit), 2)


def bit_order(devices, group_size, flipped):
    group_bits = group_size.bit_length() - 1
    total_bits = devices.bit_length() - 1
    chips = list(range(group_bits + 1, total_bits))
    if flipped:
        chips = chips[::-1]
    return [group_bits] + chips + list(range(group_bits))[::-1]


def sum_scatter(block, devices, group_size, flipped):
    left = list(range(devices.bit_length() - 1))[::-1]
    columns = block.shape[1]
    for bit in bit_order(devices, group_size, flipped):
        before = 2 ** left.index(bit)
        view = block.reshape(before, 2, -1, columns)
        own = own_bit(bit, group_size)
        kept = lax.dynamic_index_in_dim(view, own, 1, keepdims=False)
        sent = lax.dynamic_index_in_dim(view, 1 - own, 1, keepdims=False)
        left.remove(bit)
        arrived = exchange(sent, bit, devices)
        block = kept.astype(jnp.float32) + arrived.astype(jnp.float32)
        if left:
            block = block.astype(jnp.bfloat16)
        block = block.reshape(-1, columns)
    return block


def gather_rows(block, devices, group_size, flipped):
    held = []
    columns = block.shape[1]
    for bit in bit_order(devices, group_size, flipped)[::-1]:
        arrived = exchange(block, bit, devices)
        held = sorted(held + [bit], reverse=True)
        before = 2 ** held.index(bit)
        first = own_bit(bit, group_size) == 0
        low = jnp.where(first, block, arrived).reshape(before, -1, columns)
        high = jnp.where(first, arrived, block).reshape(before, -1, columns)
        block = jnp.stack([low, high], axis=1).reshape(-1, columns)
    return block


def adam_step(weight, gradient, moment_one, moment_two, decay_rate, step_rate):
    moment_one = beta_first * moment_one + (1.0 - beta_first) * gradient
    moment_two = beta_second * moment_two + (1.0 - beta_second) * gradient * gradient
    first_hat = moment_one / (1.0 - beta_first**STEP)
    second_hat = moment_two / (1.0 - beta_second**STEP)
    weight = weight - step_rate * (
        first_hat / (jnp.sqrt(second_hat) + adam_eps) + decay_rate * weight
    )
    return (weight, moment_one, moment_two)


def per_device(
    devices,
    group_size,
    tokens,
    cotangent,
    seq_lens,
    w_qkv,
    w_out,
    w_up,
    w_down,
    vectors,
    first_qkv,
    first_out,
    first_up,
    first_down,
    first_vec,
    second_qkv,
    second_out,
    second_up,
    second_down,
    second_vec,
):
    shard_rows = w_out.shape[0] // D
    low_qkv = w_qkv.astype(jnp.bfloat16).reshape(shard_rows, 3 * D)
    low_out = w_out.astype(jnp.bfloat16).reshape(shard_rows, D)
    low_up = w_up.astype(jnp.bfloat16).reshape(shard_rows, FF)
    low_down = w_down.astype(jnp.bfloat16).reshape(-1, D)
    low_vec = vectors.astype(jnp.bfloat16).reshape(shard_rows, -1)
    vec_width = low_vec.shape[1]
    vec_pad = ((0, 0), (0, 128 - vec_width))
    low_up = jnp.concatenate([low_up, jnp.pad(low_vec, vec_pad)], axis=1)
    low_late = jnp.concatenate([low_qkv[:, 2 * D :], low_out], axis=1)
    full_up = gather_rows(low_up, devices, group_size, False)
    weight_down = gather_rows(low_down, devices, group_size, True)
    full_early = gather_rows(low_qkv[:, : 2 * D], devices, group_size, False)
    full_late = gather_rows(low_late, devices, group_size, True)
    weight_up = full_up[:, :FF]
    packed = full_up[:, FF : FF + vec_width].reshape(-1).astype(jnp.float32)
    weight_qkv = jnp.concatenate([full_early, full_late[:, :D]], axis=1)
    weight_out = full_late[:, D:]
    gain_one = packed[0:D]
    gain_two = packed[D : 2 * D]
    shift_one = packed[2 * D : 3 * D]
    shift_two = packed[3 * D : 4 * D]
    bias_qkv = packed[4 * D : 7 * D]
    bias_out = packed[7 * D : 8 * D]
    bias_up = packed[8 * D : 8 * D + FF]
    bias_down = packed[8 * D + FF :]
    document, position, live_rows = packing(seq_lens[0])
    inputs = tokens.astype(jnp.float32)
    normed_one, normal_one, scaled_one = norm_parts(inputs, gain_one, shift_one)
    normed_two, normal_two, scaled_two = norm_parts(inputs, gain_two, shift_two)
    normed_one = normed_one.astype(jnp.bfloat16)
    normed_two = normed_two.astype(jnp.bfloat16)
    seed_rows = jnp.where(live_rows[:, None], cotangent, jnp.zeros_like(cotangent))
    begins = jnp.arange(TOK_DEV, dtype=jnp.int32) - position
    tables = lane_tables(position)
    parts = [
        attention(
            begins[None, :],
            normed_one,
            seed_rows,
            weight_qkv,
            bias_qkv[None, :],
            weight_out,
            tables,
            first,
            2,
        )
        for first in range(0, HEADS // 2, 2)
    ]
    context = jnp.concatenate([part[0] for part in parts], axis=1)
    grad_projected = jnp.concatenate([part[1] for part in parts], axis=1)
    attended = jnp.dot(context, weight_out, preferred_element_type=jnp.float32) + bias_out
    hidden = jnp.dot(normed_two, weight_up, preferred_element_type=jnp.float32) + bias_up
    activation, gelu_back = jax.vjp(lambda entry: jax.nn.gelu(entry, approximate=False), hidden)
    activated = activation.astype(jnp.bfloat16)
    result = (
        inputs
        + attended
        + jnp.dot(activated, weight_down, preferred_element_type=jnp.float32)
        + bias_down
    )
    seed_float = seed_rows.astype(jnp.float32)
    grad_down = jnp.einsum("tf,td->fd", activated, seed_rows, preferred_element_type=jnp.float32)
    grad_out = jnp.einsum("tc,td->cd", context, seed_rows, preferred_element_type=jnp.float32)
    grad_act = jnp.einsum("td,fd->tf", seed_rows, weight_down, preferred_element_type=jnp.float32)
    grad_hidden = gelu_back(grad_act)[0].astype(jnp.bfloat16)
    grad_up = jnp.einsum("td,tf->df", normed_two, grad_hidden, preferred_element_type=jnp.float32)
    grad_two = jnp.einsum("tf,df->td", grad_hidden, weight_up, preferred_element_type=jnp.float32)
    grad_qkv = jnp.einsum(
        "td,te->de", normed_one, grad_projected, preferred_element_type=jnp.float32
    )
    grad_one = jnp.einsum(
        "te,de->td", grad_projected, weight_qkv, preferred_element_type=jnp.float32
    )
    input_one, gain_grad_one, shift_grad_one = norm_back(grad_one, normal_one, scaled_one, gain_one)
    input_two, gain_grad_two, shift_grad_two = norm_back(grad_two, normal_two, scaled_two, gain_two)
    input_grad = seed_float + input_one + input_two
    seed_total = jnp.sum(seed_float, axis=0)
    grad_vec = jnp.concatenate(
        [
            gain_grad_one,
            gain_grad_two,
            shift_grad_one,
            shift_grad_two,
            jnp.sum(grad_projected.astype(jnp.float32), axis=0),
            seed_total,
            jnp.sum(grad_hidden.astype(jnp.float32), axis=0),
            seed_total,
        ]
    )
    grad_early = grad_qkv[:, : 2 * D].astype(jnp.bfloat16)
    grad_late = jnp.concatenate(
        [
            grad_qkv[:, 2 * D :].astype(jnp.bfloat16),
            grad_out.astype(jnp.bfloat16),
            jnp.pad(grad_vec.reshape(D, -1), vec_pad).astype(jnp.bfloat16),
        ],
        axis=1,
    )
    sum_up = sum_scatter(grad_up.astype(jnp.bfloat16), devices, group_size, False)
    sum_down = sum_scatter(grad_down.astype(jnp.bfloat16), devices, group_size, True)
    sum_early = sum_scatter(grad_early, devices, group_size, False)
    sum_late = sum_scatter(grad_late, devices, group_size, True)
    summed = (
        jnp.concatenate([sum_early, sum_late[:, :D]], axis=1).reshape(-1),
        sum_late[:, D : 2 * D].reshape(-1),
        sum_up.reshape(-1),
        sum_down.reshape(-1),
        sum_late[:, 2 * D : 2 * D + vec_width].reshape(-1),
    )
    masters = (w_qkv, w_out, w_up, w_down, vectors)
    firsts = (first_qkv, first_out, first_up, first_down, first_vec)
    seconds = (second_qkv, second_out, second_up, second_down, second_vec)
    decays = (weight_decay, weight_decay, weight_decay, weight_decay, 0.0)
    rates = (learn_rate, learn_rate, learn_rate, learn_rate, vector_rate)
    updated = [
        adam_step(weight, gradient, moment_one, moment_two, decay_rate, step_rate)
        for weight, gradient, moment_one, moment_two, decay_rate, step_rate in zip(
            masters, summed, firsts, seconds, decays, rates
        )
    ]
    return (
        result.astype(jnp.bfloat16),
        input_grad,
        updated[0][0],
        updated[1][0],
        updated[2][0],
        updated[3][0],
        updated[4][0],
        updated[0][1],
        updated[1][1],
        updated[2][1],
        updated[3][1],
        updated[4][1],
        updated[0][2],
        updated[1][2],
        updated[2][2],
        updated[3][2],
        updated[4][2],
    )


def solution(mesh):
    placed = (
        P(("dp", "group"), None),
        P(("dp", "group"), None),
        P(("dp", "group"), None),
        P(("dp", "group")),
        P(("dp", "group")),
        P(("dp", "group")),
        P(("dp", "group")),
        P(("dp", "group")),
        P(("dp", "group")),
        P(("dp", "group")),
        P(("dp", "group")),
        P(("dp", "group")),
        P(("dp", "group")),
        P(("dp", "group")),
        P(("dp", "group")),
        P(("dp", "group")),
        P(("dp", "group")),
        P(("dp", "group")),
    )
    group_size = mesh.shape["group"]
    devices = mesh.shape["dp"] * group_size
    return jax.shard_map(
        functools.partial(per_device, devices, group_size),
        mesh=mesh,
        in_specs=placed,
        out_specs=(
            P(("dp", "group"), None),
            P(("dp", "group"), None),
            P(("dp", "group")),
            P(("dp", "group")),
            P(("dp", "group")),
            P(("dp", "group")),
            P(("dp", "group")),
            P(("dp", "group")),
            P(("dp", "group")),
            P(("dp", "group")),
            P(("dp", "group")),
            P(("dp", "group")),
            P(("dp", "group")),
            P(("dp", "group")),
            P(("dp", "group")),
            P(("dp", "group")),
            P(("dp", "group")),
        ),
        check_vma=False,
    )
```
